32 devices in a mesh: bx: 8 (over y, x, core), cy: 4 (over z).
Axes of the slice: x: 2, y: 2, z: 4, core: 2. Of those that a mesh axis runs over, the one named last changes fastest.
Arguments:
- fractions: bfloat16 [8, 256, 16, 512], P(None, 'bx', None, 'cy'), may hold values from 0.05 to 1134.4, as said below
- ext_table: bfloat16 [32, 8], replicated, may hold values from 0.5 to 3.5
- side_table: bfloat16 [32, 8], replicated, may hold values from 0.049804688 to 0.59765625
- depth_scale: float32 [32], replicated, may hold values from 3.125e-05 to 0.0026666667, as said below
Outputs:
- image_out: float32 [32, 256, 16], P('cy', 'bx')
The draws below stay inside these ranges and needn't reach their ends.
Inputs may be any that keep to these rules, and one draw needn't show every extreme that they name: Positive volume fractions. `depth_scale`: positive scales.
All inputs are finite; a program needn't handle non-finite values.
Results may differ from the reference program's by a relative error of at most 0.0003.
Values sent between devices are 32-bit elements; how exact they have to be, the bound alone decides.
A program may use at most 128 MiB of HBM per device.

```python
import jax
import jax.numpy as jnp
from jax import lax

W = 32
NB = 8
CX = 32
CY = 128
NZ = 16
LASER_PATH_BINS = 256
VIEW_DEPTH_BINS = 512


def draw_depth_scale(key, part):
    key = jax.random.fold_in(key, 11)
    longest = max(LASER_PATH_BINS, VIEW_DEPTH_BINS)
    lower = jnp.log(0.5 / longest)
    upper = jnp.log(1.0 / 30.0)
    values = jnp.exp(jax.random.uniform(key, (W,), jnp.float32, lower, upper))
    return values / 12.5


def draw_fractions(key, part):
    key = jax.random.fold_in(key, 23)
    derived_seeds = jax.random.split(key, 6)
    longest = max(LASER_PATH_BINS, VIEW_DEPTH_BINS)
    base_field = jnp.exp(jax.random.uniform(derived_seeds[0], (NB, LASER_PATH_BINS, NZ, VIEW_DEPTH_BINS), jnp.float32, jnp.log(0.2), jnp.log(2.0)))
    regional = jnp.exp(jax.random.uniform(derived_seeds[1], (LASER_PATH_BINS // CX, VIEW_DEPTH_BINS // CY), jnp.float32, jnp.log(0.4), jnp.log(2.5)))
    regional = jnp.repeat(jnp.repeat(regional, CX, axis=0), CY, axis=1)
    horizontal_pulses = jax.random.randint(derived_seeds[2], (3,), 0, LASER_PATH_BINS)
    vertical_pulses = jax.random.randint(derived_seeds[3], (3,), 0, VIEW_DEPTH_BINS)
    horizontal_labels = jnp.any(jnp.arange(LASER_PATH_BINS)[:, None] == horizontal_pulses[None, :], axis=1).astype(jnp.float32)
    vertical_labels = jnp.any(jnp.arange(VIEW_DEPTH_BINS)[:, None] == vertical_pulses[None, :], axis=1).astype(jnp.float32)
    row_size = jax.random.uniform(derived_seeds[4], (NB,), jnp.float32, 0.3, 1.1) * longest
    col_size = jax.random.uniform(derived_seeds[5], (NB,), jnp.float32, 0.3, 1.1) * longest
    field = base_field * regional[None, :, None, :]
    field = field + row_size[:, None, None, None] * horizontal_labels[None, :, None, None]
    field = field + col_size[:, None, None, None] * vertical_labels[None, None, None, :]
    return field.astype(jnp.bfloat16)


def setup_inputs(seed: int = 0) -> dict:
    key_list = jax.random.split(jax.random.key(seed), 5)
    return {
        "fractions": draw_fractions(jax.random.fold_in(key_list[4], 71), 0),
        "ext_table": jnp.clip(jax.random.uniform(key_list[1], (W, NB), jnp.float32, 0.5, 3.5), 0.5, 3.5).astype(jnp.bfloat16),
        "side_table": jnp.clip(jax.random.uniform(key_list[2], (W, NB), jnp.float32, 0.049804688, 0.59765625), 0.049804688, 0.59765625).astype(jnp.bfloat16),
        "depth_scale": draw_depth_scale(jax.random.fold_in(key_list[4], 71), 0),
    }


def reference(fractions, ext_table, side_table, depth_scale):
    tables = jnp.concatenate([ext_table, side_table], axis=0)
    planes = jnp.moveaxis(fractions, 2, 0)

    def one_slice(z_plane):
        stacked = jnp.dot(tables, z_plane.reshape(NB, -1), preferred_element_type=jnp.float32)
        stacked = stacked.reshape(2 * W, LASER_PATH_BINS, VIEW_DEPTH_BINS)
        extinction = stacked[:W] * depth_scale[:, None, None]
        side_light = stacked[W:]
        beam_depth = jnp.cumsum(extinction, axis=1) - 0.5 * extinction
        camera_depth = jnp.flip(jnp.cumsum(jnp.flip(extinction, 2), axis=2), 2) - 0.5 * extinction
        return jnp.sum(side_light * jnp.exp(-(beam_depth + camera_depth)), axis=2) / VIEW_DEPTH_BINS

    images = lax.map(one_slice, planes)
    return jnp.transpose(images, (1, 2, 0))
```

```python
import functools

import jax
import jax.numpy as jnp
from jax import lax
from jax.experimental import pallas as pl
from jax.experimental.pallas import tpu as pltpu
from jax.sharding import PartitionSpec as P

LOG2E = 1.4426950408889634
MESH = pl.DeviceIdType.MESH


def split_halves(value):
    high = value.astype(jnp.bfloat16)
    low = (value - high.astype(jnp.float32)).astype(jnp.bfloat16)
    return jnp.concatenate([high, low], axis=1)


def matmul(a, b, dims=((1,), (0,))):
    return lax.dot_general(a, b, (dims, ((), ())), preferred_element_type=jnp.float32)


def kernel(
    n, m, f_hbm, ext_ref, side_ref, scale_ref, out_ref,
    f_ref, prod_ref, beam_ref, beam_in, cam_ref, cam_in, img_ref, img_out, img_in,
    ext_w, side_w, factor_ref,
    f_sem, beam_send, beam_recv, cam_send, cam_recv, img_send, img_recv,
):
    nb, cx, nz, cy = f_ref.shape
    w = ext_ref.shape[1]
    bz, wz = nb * nz, w * nz
    bx_me, cy_me = lax.axis_index("bx"), lax.axis_index("cy")

    load = pltpu.make_async_copy(f_hbm, f_ref, f_sem)
    load.start()

    barrier = pltpu.get_barrier_semaphore()

    def greet_bx(t, c):
        pl.semaphore_signal(barrier, inc=1, device_id={"bx": t}, device_id_type=MESH)
        return c

    def greet_cy(t, c):
        @pl.when(t != cy_me)
        def _():
            pl.semaphore_signal(barrier, inc=1, device_id={"cy": t}, device_id_type=MESH)
        return c

    lax.fori_loop(0, bx_me, greet_bx, 0)
    lax.fori_loop(0, m, greet_cy, 0)

    i32, bf16, f32 = jnp.int32, jnp.bfloat16, jnp.float32
    lane_w = lax.broadcasted_iota(i32, (w, wz), 1) // nz
    spread = (lane_w == lax.broadcasted_iota(i32, (w, wz), 0)).astype(f32)
    row_b = lax.broadcasted_iota(i32, (bz, nb), 0) // nz
    rows = (row_b == lax.broadcasted_iota(i32, (bz, nb), 1)).astype(f32).astype(bf16)
    same_z = (
        lax.broadcasted_iota(i32, (bz, wz), 0) % nz
        == lax.broadcasted_iota(i32, (bz, wz), 1) % nz
    )
    spread16 = spread.astype(bf16)

    def table(ref):
        wide = matmul(rows, matmul(ref[...], spread16).astype(bf16))
        return jnp.where(same_z, wide, 0.0).astype(bf16)

    ext = table(ext_ref)
    ext_w[:bz] = ext
    ext_w[bz:] = ext
    side_w[...] = table(side_ref)
    scale = lax.dot_general(
        jnp.broadcast_to(scale_ref[...], (8, w)), spread, (((1,), (0,)), ((), ())),
        precision=lax.Precision.HIGHEST, preferred_element_type=f32,
    )
    factor_ref[...] = scale * (-LOG2E)

    load.wait()

    def add_x(x, total):
        return total + f_ref[:, x].astype(f32)

    total = lax.fori_loop(0, cx, add_x, jnp.zeros((nb, nz, cy), f32), unroll=4)
    beam_ref[...] = total.reshape(bz, cy)

    pl.semaphore_wait(barrier, n - 1 - bx_me + m - 1)

    def beam_copy(slot, t):
        return pltpu.make_async_remote_copy(
            src_ref=beam_ref, dst_ref=beam_in.at[slot],
            send_sem=beam_send.at[t], recv_sem=beam_recv.at[slot],
            device_id={"bx": t}, device_id_type=MESH,
        )

    def beam_start(t, c):
        beam_copy(bx_me, t).start()
        return c

    lax.fori_loop(bx_me + 1, n, beam_start, 0)

    r = lax.broadcasted_iota(i32, (2 * cy, cy), 0)
    y = lax.broadcasted_iota(i32, (2 * cy, cy), 1)
    above = jnp.where(y >= r, 1.0, 0.0)
    sums = jnp.where(r < cy, above, jnp.where(y == r - cy, 1.0, 0.0)).astype(bf16)

    def two_x(i, before):
        pair = jnp.concatenate(
            [f_ref[:, 2 * i].reshape(bz, cy), f_ref[:, 2 * i + 1].reshape(bz, cy)], axis=0
        )
        both = matmul(sums, pair, ((1,), (1,)))
        for k in range(2):
            x = 2 * i + k
            camera = both[:cy, k * bz:(k + 1) * bz]
            cells = both[cy:, k * bz:(k + 1) * bz]
            cam_ref[pl.ds(x, 1), :] = camera[:1]
            depth = matmul(split_halves(camera + before), ext_w[...])
            light = matmul(cells.astype(bf16), side_w[...])
            prod_ref[x] = light * jnp.exp2(depth * factor_ref[:1])
            before = before + cells
        return before

    lax.fori_loop(0, cx // 2, two_x, jnp.zeros((cy, bz), f32))

    def cam_copy(slot, t):
        return pltpu.make_async_remote_copy(
            src_ref=cam_ref, dst_ref=cam_in.at[slot],
            send_sem=cam_send.at[t], recv_sem=cam_recv.at[slot],
            device_id={"cy": t}, device_id_type=MESH,
        )

    def cam_start(t, c):
        cam_copy(cy_me, t).start()
        return c

    lax.fori_loop(0, cy_me, cam_start, 0)

    def beam_add(j, total):
        beam_copy(j, j).wait_recv()
        return total + beam_in[j]

    beam = lax.fori_loop(0, bx_me, beam_add, jnp.zeros((bz, cy), f32))
    beam_depth = matmul(split_halves(beam.T), ext_w[...])
    beam_factor = jnp.exp2(beam_depth * factor_ref[:1])
    prod_dim = 128
    for lane in range(0, wz, prod_dim):
        lanes = slice(lane, lane + prod_dim)
        part = beam_factor[:, lanes]

        def eight_x(g, c):
            first = pl.multiple_of(8 * g, 8)
            rows8 = [
                jnp.sum(prod_ref[first + k, :, lanes] * part, axis=0, keepdims=True)
                for k in range(8)
            ]
            img_ref[pl.ds(first, 8), lanes] = jnp.concatenate(rows8, axis=0)
            return c

        lax.fori_loop(0, cx // 8, eight_x, 0)

    def cam_add(j, total):
        cam_copy(j, j).wait_recv()
        return total + cam_in[j]

    cam = lax.fori_loop(cy_me + 1, m, cam_add, jnp.zeros((cx, bz), f32))
    cam_depth = matmul(split_halves(cam), ext_w[...])
    image = img_ref[...] * jnp.exp2(cam_depth * factor_ref[:1]) * (1.0 / (cy * m))
    width = wz // m
    for j in range(m):
        img_out[j] = image[:, j * width:(j + 1) * width]

    def img_copy(block, slot, t):
        return pltpu.make_async_remote_copy(
            src_ref=img_out.at[block], dst_ref=img_in.at[slot],
            send_sem=img_send.at[t], recv_sem=img_recv.at[slot],
            device_id={"cy": t}, device_id_type=MESH,
        )

    def img_start(t, c):
        @pl.when(t != cy_me)
        def _():
            img_copy(t, cy_me, t).start()
        return c

    lax.fori_loop(0, m, img_start, 0)
    out_ref[...] = img_out[cy_me]

    def img_add(j, c):
        @pl.when(j != cy_me)
        def _():
            img_copy(j, j, j).wait_recv()
            out_ref[...] += img_in[j]
        return c

    lax.fori_loop(0, m, img_add, 0)

    def beam_sent(t, c):
        beam_copy(bx_me, t).wait_send()
        return c

    def cam_sent(t, c):
        cam_copy(cy_me, t).wait_send()
        return c

    def img_sent(t, c):
        @pl.when(t != cy_me)
        def _():
            img_copy(t, cy_me, t).wait_send()
        return c

    lax.fori_loop(bx_me + 1, n, beam_sent, 0)
    lax.fori_loop(0, cy_me, cam_sent, 0)
    lax.fori_loop(0, m, img_sent, 0)


def on_device(n, m, fractions, ext_table, side_table, depth_scale):
    nb, cx, nz, cy = fractions.shape
    w = ext_table.shape[0]
    bz, wz = nb * nz, w * nz
    width = wz // m
    f32, bf16 = jnp.float32, jnp.bfloat16
    dma = pltpu.SemaphoreType.DMA
    vmem = pl.BlockSpec(memory_space=pltpu.VMEM)
    image = pl.pallas_call(
        functools.partial(kernel, n, m),
        out_shape=jax.ShapeDtypeStruct((cx, width), f32),
        in_specs=[pl.BlockSpec(memory_space=pl.ANY), vmem, vmem, vmem],
        out_specs=vmem,
        scratch_shapes=[
            pltpu.VMEM((nb, cx, nz, cy), bf16),
            pltpu.VMEM((cx, cy, wz), f32),
            pltpu.VMEM((bz, cy), f32),
            pltpu.VMEM((n, bz, cy), f32),
            pltpu.VMEM((cx, bz), f32),
            pltpu.VMEM((m, cx, bz), f32),
            pltpu.VMEM((cx, wz), f32),
            pltpu.VMEM((m, cx, width), f32),
            pltpu.VMEM((m, cx, width), f32),
            pltpu.VMEM((2 * bz, wz), bf16),
            pltpu.VMEM((bz, wz), bf16),
            pltpu.VMEM((8, wz), f32),
            dma, dma((n,)), dma((n,)), dma((m,)), dma((m,)), dma((m,)), dma((m,)),
        ],
        compiler_params=pltpu.CompilerParams(
            collective_id=0, has_side_effects=True, vmem_limit_bytes=40 * 1024 * 1024
        ),
    )(fractions, ext_table.T, side_table.T, depth_scale.reshape(1, w))
    return jnp.transpose(image.reshape(cx, w // m, nz), (1, 0, 2))


def solution(mesh):
    return jax.shard_map(
        functools.partial(on_device, mesh.shape["bx"], mesh.shape["cy"]),
        mesh=mesh,
        in_specs=(P(None, "bx", None, "cy"), P(), P(), P()),
        out_specs=P("cy", "bx", None),
        check_vma=False,
    )
```

```python
import functools

import jax
import jax.numpy as jnp
from jax import lax
from jax.experimental import pallas as pl
from jax.experimental.pallas import tpu as pltpu
from jax.sharding import PartitionSpec as P

LOG2E = 1.4426950408889634
MESH = pl.DeviceIdType.MESH
GROUP = 8
EARLY = 0
FIRST = 1
SECOND = 2
THIRD = 3


def split_halves(value):
    high = value.astype(jnp.bfloat16)
    low = (value - high.astype(jnp.float32)).astype(jnp.bfloat16)
    return jnp.concatenate([high, low], axis=1)


def matmul(a, b, dims=((1,), (0,))):
    return lax.dot_general(a, b, (dims, ((), ())), preferred_element_type=jnp.float32)


def kernel(
    n, m, f_hbm, ext_hbm, side_hbm, scale_hbm, out_ref,
    f_ref, ext_ref, side_ref, scale_ref, prod_ref, beam_ref, mate_in, pair_ref, pair_in, ahead_ref, ahead_in, cam_ref, cam_in, img_ref, img_out, img_in,
    ext_w, side_w, factor_ref,
    f_sem, table_sem, mate_sem, ahead_sem, pair_send, pair_recv, cam_send, cam_recv, img_send, img_recv,
):
    nb, cx, nz, cy = f_ref.shape
    w = ext_ref.shape[1]
    bz, wz = nb * nz, w * nz
    bx_me, cy_me = lax.axis_index("bx"), lax.axis_index("cy")


    barrier = pltpu.get_barrier_semaphore()

    half, pair, pairs = bx_me % 2, bx_me // 2, n // 2
    mate = 2 * pair + 1 - half

    def greet_bx(t, c):
        pl.semaphore_signal(
            barrier, inc=1, device_id={"bx": 2 * t + half}, device_id_type=MESH
        )
        return c

    pl.semaphore_signal(barrier, inc=1, device_id={"bx": mate}, device_id_type=MESH)

    def greet_cy(t, c):
        @pl.when(t != cy_me)
        def _():
            pl.semaphore_signal(barrier, inc=1, device_id={"cy": t}, device_id_type=MESH)
        return c

    lax.fori_loop(0, pair, greet_bx, 0)
    lax.fori_loop(0, m, greet_cy, 0)

    loads = [
        pltpu.make_async_copy(src, dst, table_sem.at[k])
        for k, (src, dst) in enumerate(
            ((ext_hbm, ext_ref), (side_hbm, side_ref), (scale_hbm, scale_ref))
        )
    ]
    load = pltpu.make_async_copy(f_hbm, f_ref, f_sem)
    for copy in (*loads, load):
        copy.start()

    i32, bf16, f32 = jnp.int32, jnp.bfloat16, jnp.float32
    lane_w = lax.broadcasted_iota(i32, (w, wz), 1) // nz
    spread = (lane_w == lax.broadcasted_iota(i32, (w, wz), 0)).astype(f32)
    row_b = lax.broadcasted_iota(i32, (bz, nb), 0) // nz
    rows = (row_b == lax.broadcasted_iota(i32, (bz, nb), 1)).astype(f32).astype(bf16)
    same_z = (
        lax.broadcasted_iota(i32, (bz, wz), 0) % nz
        == lax.broadcasted_iota(i32, (bz, wz), 1) % nz
    )
    spread16 = spread.astype(bf16)

    for copy in loads:
        copy.wait()

    def table(ref):
        wide = matmul(rows, matmul(ref[...], spread16).astype(bf16))
        return jnp.where(same_z, wide, 0.0).astype(bf16)

    ext = table(ext_ref)
    ext_w[:bz] = ext
    ext_w[bz:] = ext
    side_w[...] = table(side_ref)
    scale = lax.dot_general(
        jnp.broadcast_to(scale_ref[...], (8, w)), spread, (((1,), (0,)), ((), ())),
        precision=lax.Precision.HIGHEST, preferred_element_type=f32,
    )
    factor_ref[...] = scale * (-LOG2E)

    load.wait()

    def add_x(x, total):
        return total + f_ref[:, x].astype(f32)

    total = lax.fori_loop(0, cx, add_x, jnp.zeros((nb, nz, cy), f32), unroll=4)
    beam_ref[...] = total.reshape(2, bz // 2, cy)

    r = lax.broadcasted_iota(i32, (2 * cy, cy), 0)
    y = lax.broadcasted_iota(i32, (2 * cy, cy), 1)
    above = jnp.where(y >= r, 1.0, 0.0)
    sums = jnp.where(r < cy, above, jnp.where(y == r - cy, 1.0, 0.0)).astype(bf16)

    ones = jnp.ones((8, cy), bf16)
    for x in range(cx):
        to_camera = matmul(ones, f_ref[:, x].reshape(bz, cy), ((1,), (1,)))
        cam_ref[x:x + 1, :] = to_camera[:1]

    def group(i, before, fused=False):
        first = i * GROUP
        depths, lights = [], []
        for k in range(0, GROUP, 2):
            pair = jnp.concatenate(
                [f_ref[:, first + k].reshape(bz, cy), f_ref[:, first + k + 1].reshape(bz, cy)],
                axis=0,
            )
            both = matmul(sums, pair, ((1,), (1,)))
            for lanes in (slice(0, bz), slice(bz, 2 * bz)):
                cells = both[cy:, lanes]
                depths.append(split_halves(both[:cy, lanes] + before))
                lights.append(cells.astype(bf16))
                before = before + cells
        depth = matmul(jnp.concatenate(depths, axis=0), ext_w[...])
        light = matmul(jnp.concatenate(lights, axis=0), side_w[...])
        product = (light * jnp.exp2(depth * factor_ref[:1])).reshape(GROUP, cy, wz)
        if fused:
            image = jnp.sum(product, axis=1)
            img_ref[pl.ds(pl.multiple_of(first, GROUP), GROUP)] = image
        else:
            prod_ref[pl.ds(first, GROUP)] = product
        return before

    steps = cx // GROUP
    early = EARLY
    before = lax.fori_loop(0, early, group, jnp.zeros((cy, bz), f32))

    pl.semaphore_wait(barrier, pairs - 1 - pair + m)

    def to_mate(src, dst, sem):
        return pltpu.make_async_remote_copy(
            src_ref=src, dst_ref=dst, send_sem=sem.at[0], recv_sem=sem.at[1],
            device_id={"bx": mate}, device_id_type=MESH,
        )

    def pair_copy(slot, t):
        return pltpu.make_async_remote_copy(
            src_ref=pair_ref, dst_ref=pair_in.at[slot],
            send_sem=pair_send.at[t], recv_sem=pair_recv.at[slot],
            device_id={"bx": 2 * t + half}, device_id_type=MESH,
        )

    mate_copy = to_mate(beam_ref.at[1 - half], mate_in, mate_sem)
    mate_copy.start()

    def cam_copy(slot, t):
        return pltpu.make_async_remote_copy(
            src_ref=cam_ref, dst_ref=cam_in.at[slot],
            send_sem=cam_send.at[t], recv_sem=cam_recv.at[slot],
            device_id={"cy": t}, device_id_type=MESH,
        )

    def cam_start(t, c):
        cam_copy(cy_me, t).start()
        return c

    lax.fori_loop(0, cy_me, cam_start, 0)

    before = lax.fori_loop(early, FIRST, group, before)

    mate_copy.wait_recv()
    pair_ref[...] = beam_ref[half] + mate_in[...]

    def pair_start(t, c):
        pair_copy(pair, t).start()
        return c

    lax.fori_loop(pair + 1, pairs, pair_start, 0)
    before = lax.fori_loop(FIRST, SECOND, group, before)

    def pair_add(j, total):
        pair_copy(j, j).wait_recv()
        return total + pair_in[j]

    mine = lax.fori_loop(0, pair, pair_add, jnp.zeros((bz // 2, cy), f32))
    second = jnp.where(half == 1, 1.0, 0.0)
    ahead_ref[...] = mine + (1.0 - second) * beam_ref[half]
    ahead_copy = to_mate(ahead_ref, ahead_in, ahead_sem)
    ahead_copy.start()
    before = lax.fori_loop(SECOND, THIRD, group, before)
    mine = mine + second * mate_in[...]
    ahead_copy.wait_recv()
    other = ahead_in[...]
    beam = jnp.concatenate(
        [jnp.where(half == 0, mine, other), jnp.where(half == 0, other, mine)], axis=0
    )
    def cam_add(j, total):
        cam_copy(j, j).wait_recv()
        return total + cam_in[j]

    cam = lax.fori_loop(cy_me + 1, m, cam_add, jnp.zeros((cx, bz), f32))
    cam_depth = matmul(split_halves(cam), ext_w[...])
    cam_factor = jnp.exp2(cam_depth * factor_ref[:1]) * (1.0 / (cy * m))
    width = wz // m
    edge = cx // 2

    def img_copy(part, block, slot, t):
        return pltpu.make_async_remote_copy(
            src_ref=img_out.at[part, block], dst_ref=img_in.at[part, slot],
            send_sem=img_send.at[part, t], recv_sem=img_recv.at[part, slot],
            device_id={"cy": t}, device_id_type=MESH,
        )

    def img_start(part):
        rows_x = slice(part * edge, (part + 1) * edge)
        image = img_ref[rows_x] * cam_factor[rows_x]
        for j in range(m):
            img_out[part, j] = image[:, j * width:(j + 1) * width]

        def one(t, c):
            @pl.when(t != cy_me)
            def _():
                img_copy(part, t, cy_me, t).start()
            return c

        lax.fori_loop(0, m, one, 0)

    beam_t = beam.T
    lax.fori_loop(
        THIRD, steps, functools.partial(group, fused=True), before + beam_t
    )
    beam_depth = matmul(split_halves(beam_t), ext_w[...])
    beam_factor = jnp.exp2(beam_depth * factor_ref[:1])

    def finish(start, stop):
        for lane in range(0, wz, 128):
            lanes = slice(lane, lane + 128)
            part = beam_factor[:, lanes]

            def eight_x(g, c):
                first = pl.multiple_of(8 * g, 8)
                rows8 = [
                    jnp.sum(prod_ref[first + k, :, lanes] * part, axis=0, keepdims=True)
                    for k in range(8)
                ]
                img_ref[pl.ds(first, 8), lanes] = jnp.concatenate(rows8, axis=0)
                return c

            lax.fori_loop(start // 8, stop // 8, eight_x, 0)

    if THIRD * GROUP > edge:
        finish(edge, THIRD * GROUP)
    img_start(1)
    finish(0, min(edge, THIRD * GROUP))
    img_start(0)
    total_ref = img_out.at[:, cy_me]

    def img_add(j, c):
        @pl.when(j != cy_me)
        def _():
            for part in (1, 0):
                img_copy(part, j, j, j).wait_recv()
            total_ref[...] += img_in[:, j]
        return c

    lax.fori_loop(0, m, img_add, 0)
    image = total_ref[...].reshape(cx, width)
    out_ref[...] = image.T.reshape(out_ref.shape)

    def pair_sent(t, c):
        pair_copy(pair, t).wait_send()
        return c

    mate_copy.wait_send()
    ahead_copy.wait_send()
    def cam_sent(t, c):
        cam_copy(cy_me, t).wait_send()
        return c

    def img_sent(t, c):
        @pl.when(t != cy_me)
        def _():
            for part in range(2):
                img_copy(part, t, cy_me, t).wait_send()
        return c

    lax.fori_loop(pair + 1, pairs, pair_sent, 0)
    lax.fori_loop(0, cy_me, cam_sent, 0)
    lax.fori_loop(0, m, img_sent, 0)


def on_device(n, m, fractions, ext_table, side_table, depth_scale):
    nb, cx, nz, cy = fractions.shape
    w = ext_table.shape[0]
    bz, wz = nb * nz, w * nz
    width = wz // m
    f32, bf16 = jnp.float32, jnp.bfloat16
    dma = pltpu.SemaphoreType.DMA
    vmem = pl.BlockSpec(memory_space=pltpu.VMEM)
    image = pl.pallas_call(
        functools.partial(kernel, n, m),
        out_shape=jax.ShapeDtypeStruct((w // m, nz, cx), f32),
        in_specs=[pl.BlockSpec(memory_space=pltpu.HBM)] * 4,
        out_specs=vmem,
        scratch_shapes=[
            pltpu.VMEM((nb, cx, nz, cy), bf16),
            pltpu.VMEM((nb, w), bf16),
            pltpu.VMEM((nb, w), bf16),
            pltpu.VMEM((1, w), f32),
            pltpu.VMEM((cx, cy, wz), f32),
            pltpu.VMEM((2, bz // 2, cy), f32),
            pltpu.VMEM((bz // 2, cy), f32),
            pltpu.VMEM((bz // 2, cy), f32),
            pltpu.VMEM((n // 2, bz // 2, cy), f32),
            pltpu.VMEM((bz // 2, cy), f32),
            pltpu.VMEM((bz // 2, cy), f32),
            pltpu.VMEM((cx, bz), f32),
            pltpu.VMEM((m, cx, bz), f32),
            pltpu.VMEM((cx, wz), f32),
            pltpu.VMEM((2, m, cx // 2, width), f32),
            pltpu.VMEM((2, m, cx // 2, width), f32),
            pltpu.VMEM((2 * bz, wz), bf16),
            pltpu.VMEM((bz, wz), bf16),
            pltpu.VMEM((8, wz), f32),
            dma, dma((3,)), dma((2,)), dma((2,)), dma((n // 2,)), dma((n // 2,)), dma((m,)), dma((m,)), dma((2, m)), dma((2, m)),
        ],
        compiler_params=pltpu.CompilerParams(
            collective_id=0, has_side_effects=True, vmem_limit_bytes=54400 * 1024
        ),
    )(fractions, ext_table.T, side_table.T, depth_scale.reshape(1, w))
    return jnp.transpose(image, (0, 2, 1))


def solution(mesh):
    return jax.shard_map(
        functools.partial(on_device, mesh.shape["bx"], mesh.shape["cy"]),
        mesh=mesh,
        in_specs=(P(None, "bx", None, "cy"), P(), P(), P()),
        out_specs=P("cy", "bx", None),
        check_vma=False,
    )
```

```python
import functools

import jax
import jax.numpy as jnp
from jax import lax
from jax.experimental import pallas as pl
from jax.experimental.pallas import tpu as pltpu
from jax.sharding import PartitionSpec as P

LOG2E = 1.4426950408889634
MESH = pl.DeviceIdType.MESH
GROUP = 8
EARLY = 0
FIRST = 1
SECOND = 3
THIRD = 4
PARTS = 4


def split_halves(value):
    high = value.astype(jnp.bfloat16)
    low = (value - high.astype(jnp.float32)).astype(jnp.bfloat16)
    return jnp.concatenate([high, low], axis=1)


def matmul(a, b, dims=((1,), (0,))):
    return lax.dot_general(a, b, (dims, ((), ())), preferred_element_type=jnp.float32)


def kernel(
    n, m, f_hbm, ext_hbm, side_hbm, scale_hbm, out_ref,
    f_ref, ext_ref, side_ref, scale_ref, prod_ref, beam_ref, mate_in, pair_ref, pair_in, ahead_ref, ahead_in, cam_ref, cam_in, img_ref, img_out, img_in,
    ext_w, side_w, factor_ref,
    f_sem, table_sem, mate_sem, ahead_sem, pair_send, pair_recv, cam_send, cam_recv, img_send, img_recv,
):
    nb, cx, nz, cy = f_ref.shape
    w = ext_ref.shape[1]
    bz, wz = nb * nz, w * nz
    bx_me, cy_me = lax.axis_index("bx"), lax.axis_index("cy")


    barrier = pltpu.get_barrier_semaphore()

    half, pair, pairs = bx_me % 2, bx_me // 2, n // 2
    mate = 2 * pair + 1 - half

    def greet_bx(t, c):
        pl.semaphore_signal(
            barrier, inc=1, device_id={"bx": 2 * t + half}, device_id_type=MESH
        )
        return c

    pl.semaphore_signal(barrier, inc=1, device_id={"bx": mate}, device_id_type=MESH)

    def greet_cy(t, c):
        @pl.when(t != cy_me)
        def _():
            pl.semaphore_signal(barrier, inc=1, device_id={"cy": t}, device_id_type=MESH)
        return c

    lax.fori_loop(0, pair, greet_bx, 0)
    lax.fori_loop(0, m, greet_cy, 0)

    loads = [
        pltpu.make_async_copy(src, dst, table_sem.at[k])
        for k, (src, dst) in enumerate(
            ((ext_hbm, ext_ref), (side_hbm, side_ref), (scale_hbm, scale_ref))
        )
    ]
    load = pltpu.make_async_copy(f_hbm, f_ref, f_sem)
    for copy in (*loads, load):
        copy.start()

    i32, bf16, f32 = jnp.int32, jnp.bfloat16, jnp.float32
    lane_w = lax.broadcasted_iota(i32, (w, wz), 1) // nz
    spread = (lane_w == lax.broadcasted_iota(i32, (w, wz), 0)).astype(f32)
    row_b = lax.broadcasted_iota(i32, (bz, nb), 0) // nz
    rows = (row_b == lax.broadcasted_iota(i32, (bz, nb), 1)).astype(f32).astype(bf16)
    same_z = (
        lax.broadcasted_iota(i32, (bz, wz), 0) % nz
        == lax.broadcasted_iota(i32, (bz, wz), 1) % nz
    )
    spread16 = spread.astype(bf16)

    for copy in loads:
        copy.wait()

    def table(ref):
        wide = matmul(rows, matmul(ref[...], spread16).astype(bf16))
        return jnp.where(same_z, wide, 0.0).astype(bf16)

    ext = table(ext_ref)
    ext_w[:bz] = ext
    ext_w[bz:] = ext
    side_w[...] = table(side_ref)
    scale = lax.dot_general(
        jnp.broadcast_to(scale_ref[...], (8, w)), spread, (((1,), (0,)), ((), ())),
        precision=lax.Precision.HIGHEST, preferred_element_type=f32,
    )
    factor_ref[...] = scale * (-LOG2E)

    load.wait()

    def add_x(x, total):
        return total + f_ref[:, x].astype(f32)

    total = lax.fori_loop(0, cx, add_x, jnp.zeros((nb, nz, cy), f32), unroll=4)
    beam_ref[...] = total.reshape(2, bz // 2, cy)

    r = lax.broadcasted_iota(i32, (2 * cy, cy), 0)
    y = lax.broadcasted_iota(i32, (2 * cy, cy), 1)
    above = jnp.where(y >= r, 1.0, 0.0)
    sums = jnp.where(r < cy, above, jnp.where(y == r - cy, 1.0, 0.0)).astype(bf16)

    ones = jnp.ones((8, cy), bf16)
    for x in range(cx):
        to_camera = matmul(ones, f_ref[:, x].reshape(bz, cy), ((1,), (1,)))
        cam_ref[x:x + 1, :] = to_camera[:1]

    def group(i, before, fused=False):
        first = i * GROUP
        depths, lights = [], []
        for k in range(0, GROUP, 2):
            pair = jnp.concatenate(
                [f_ref[:, first + k].reshape(bz, cy), f_ref[:, first + k + 1].reshape(bz, cy)],
                axis=0,
            )
            both = matmul(sums, pair, ((1,), (1,)))
            for lanes in (slice(0, bz), slice(bz, 2 * bz)):
                cells = both[cy:, lanes]
                depths.append(split_halves(both[:cy, lanes] + before))
                lights.append(cells.astype(bf16))
                before = before + cells
        depth = matmul(jnp.concatenate(depths, axis=0), ext_w[...])
        light = matmul(jnp.concatenate(lights, axis=0), side_w[...])
        product = (light * jnp.exp2(depth * factor_ref[:1])).reshape(GROUP, cy, wz)
        if fused:
            image = jnp.sum(product, axis=1)
            img_ref[pl.ds(pl.multiple_of(first, GROUP), GROUP)] = image
        else:
            prod_ref[pl.ds(first, GROUP)] = product
        return before

    steps = cx // GROUP
    early = EARLY
    before = lax.fori_loop(0, early, group, jnp.zeros((cy, bz), f32))

    pl.semaphore_wait(barrier, pairs - 1 - pair + m)

    def to_mate(src, dst, sem):
        return pltpu.make_async_remote_copy(
            src_ref=src, dst_ref=dst, send_sem=sem.at[0], recv_sem=sem.at[1],
            device_id={"bx": mate}, device_id_type=MESH,
        )

    def pair_copy(slot, t):
        return pltpu.make_async_remote_copy(
            src_ref=pair_ref, dst_ref=pair_in.at[slot],
            send_sem=pair_send.at[t], recv_sem=pair_recv.at[slot],
            device_id={"bx": 2 * t + half}, device_id_type=MESH,
        )

    mate_copy = to_mate(beam_ref.at[1 - half], mate_in, mate_sem)
    mate_copy.start()

    def cam_copy(slot, t):
        return pltpu.make_async_remote_copy(
            src_ref=cam_ref, dst_ref=cam_in.at[slot],
            send_sem=cam_send.at[t], recv_sem=cam_recv.at[slot],
            device_id={"cy": t}, device_id_type=MESH,
        )

    def cam_start(t, c):
        cam_copy(cy_me, t).start()
        return c

    lax.fori_loop(0, cy_me, cam_start, 0)

    before = lax.fori_loop(early, FIRST, group, before)

    mate_copy.wait_recv()
    pair_ref[...] = beam_ref[half] + mate_in[...]

    def pair_start(t, c):
        pair_copy(pair, pairs + pair - t).start()
        return c

    lax.fori_loop(pair + 1, pairs, pair_start, 0)
    before = lax.fori_loop(FIRST, SECOND, group, before)

    def pair_add(j, total):
        pair_copy(j, j).wait_recv()
        return total + pair_in[j]

    mine = lax.fori_loop(0, pair, pair_add, jnp.zeros((bz // 2, cy), f32))
    second = jnp.where(half == 1, 1.0, 0.0)
    ahead_ref[...] = mine + (1.0 - second) * beam_ref[half]
    ahead_copy = to_mate(ahead_ref, ahead_in, ahead_sem)
    ahead_copy.start()
    before = lax.fori_loop(SECOND, THIRD, group, before)
    mine = mine + second * mate_in[...]
    ahead_copy.wait_recv()
    other = ahead_in[...]
    beam = jnp.concatenate(
        [jnp.where(half == 0, mine, other), jnp.where(half == 0, other, mine)], axis=0
    )
    def cam_add(j, total):
        cam_copy(j, j).wait_recv()
        return total + cam_in[j]

    cam = lax.fori_loop(cy_me + 1, m, cam_add, jnp.zeros((cx, bz), f32))
    cam_depth = matmul(split_halves(cam), ext_w[...])
    cam_factor = jnp.exp2(cam_depth * factor_ref[:1]) * (1.0 / (cy * m))
    width = wz // m
    edge = cx // PARTS

    def img_copy(part, block, slot, t):
        return pltpu.make_async_remote_copy(
            src_ref=img_out.at[part, block], dst_ref=img_in.at[part, slot],
            send_sem=img_send.at[part, t], recv_sem=img_recv.at[part, slot],
            device_id={"cy": t}, device_id_type=MESH,
        )

    def img_start(part):
        rows_x = slice(part * edge, (part + 1) * edge)
        image = img_ref[rows_x] * cam_factor[rows_x]
        for j in range(m):
            img_out[part, j] = image[:, j * width:(j + 1) * width]

        def one(t, c):
            @pl.when(t != cy_me)
            def _():
                img_copy(part, t, cy_me, t).start()
            return c

        lax.fori_loop(0, m, one, 0)

    beam_t = beam.T
    lax.fori_loop(
        THIRD, steps, functools.partial(group, fused=True), before + beam_t
    )
    beam_depth = matmul(split_halves(beam_t), ext_w[...])
    beam_factor = jnp.exp2(beam_depth * factor_ref[:1])

    def finish(start, stop):
        for lane in range(0, wz, 128):
            lanes = slice(lane, lane + 128)
            part = beam_factor[:, lanes]

            def eight_x(g, c):
                first = pl.multiple_of(8 * g, 8)
                rows8 = [
                    jnp.sum(prod_ref[first + k, :, lanes] * part, axis=0, keepdims=True)
                    for k in range(8)
                ]
                img_ref[pl.ds(first, 8), lanes] = jnp.concatenate(rows8, axis=0)
                return c

            lax.fori_loop(start // 8, max(start, stop) // 8, eight_x, 0)

    for part in reversed(range(PARTS)):
        finish(part * edge, min((part + 1) * edge, THIRD * GROUP))
        img_start(part)
    total_ref = img_out.at[:, cy_me]

    def img_add(j, c):
        @pl.when(j != cy_me)
        def _():
            for part in reversed(range(PARTS)):
                img_copy(part, j, j, j).wait_recv()
            total_ref[...] += img_in[:, j]
        return c

    lax.fori_loop(0, m, img_add, 0)
    image = total_ref[...].reshape(cx, width)
    out_ref[...] = image.T.reshape(out_ref.shape)

    def pair_sent(t, c):
        pair_copy(pair, t).wait_send()
        return c

    mate_copy.wait_send()
    ahead_copy.wait_send()
    def cam_sent(t, c):
        cam_copy(cy_me, t).wait_send()
        return c

    def img_sent(t, c):
        @pl.when(t != cy_me)
        def _():
            for part in range(PARTS):
                img_copy(part, t, cy_me, t).wait_send()
        return c

    lax.fori_loop(pair + 1, pairs, pair_sent, 0)
    lax.fori_loop(0, cy_me, cam_sent, 0)
    lax.fori_loop(0, m, img_sent, 0)


def on_device(n, m, fractions, ext_table, side_table, depth_scale):
    nb, cx, nz, cy = fractions.shape
    w = ext_table.shape[0]
    bz, wz = nb * nz, w * nz
    width = wz // m
    f32, bf16 = jnp.float32, jnp.bfloat16
    dma = pltpu.SemaphoreType.DMA
    vmem = pl.BlockSpec(memory_space=pltpu.VMEM)
    image = pl.pallas_call(
        functools.partial(kernel, n, m),
        out_shape=jax.ShapeDtypeStruct((w // m, nz, cx), f32),
        in_specs=[pl.BlockSpec(memory_space=pltpu.HBM)] * 4,
        out_specs=vmem,
        scratch_shapes=[
            pltpu.VMEM((nb, cx, nz, cy), bf16),
            pltpu.VMEM((nb, w), bf16),
            pltpu.VMEM((nb, w), bf16),
            pltpu.VMEM((1, w), f32),
            pltpu.VMEM((cx, cy, wz), f32),
            pltpu.VMEM((2, bz // 2, cy), f32),
            pltpu.VMEM((bz // 2, cy), f32),
            pltpu.VMEM((bz // 2, cy), f32),
            pltpu.VMEM((n // 2, bz // 2, cy), f32),
            pltpu.VMEM((bz // 2, cy), f32),
            pltpu.VMEM((bz // 2, cy), f32),
            pltpu.VMEM((cx, bz), f32),
            pltpu.VMEM((m, cx, bz), f32),
            pltpu.VMEM((cx, wz), f32),
            pltpu.VMEM((PARTS, m, cx // PARTS, width), f32),
            pltpu.VMEM((PARTS, m, cx // PARTS, width), f32),
            pltpu.VMEM((2 * bz, wz), bf16),
            pltpu.VMEM((bz, wz), bf16),
            pltpu.VMEM((8, wz), f32),
            dma, dma((3,)), dma((2,)), dma((2,)), dma((n // 2,)), dma((n // 2,)), dma((m,)), dma((m,)), dma((PARTS, m)), dma((PARTS, m)),
        ],
        compiler_params=pltpu.CompilerParams(
            collective_id=0, has_side_effects=True, vmem_limit_bytes=54400 * 1024
        ),
    )(fractions, ext_table.T, side_table.T, depth_scale.reshape(1, w))
    return jnp.transpose(image, (0, 2, 1))


def solution(mesh):
    return jax.shard_map(
        functools.partial(on_device, mesh.shape["bx"], mesh.shape["cy"]),
        mesh=mesh,
        in_specs=(P(None, "bx", None, "cy"), P(), P(), P()),
        out_specs=P("cy", "bx", None),
        check_vma=False,
    )
```
